256 devices in a mesh: dp: 2 (over x_hi), qrow: 16 (over z, core), kcol: 8 (over x_lo, y).
Axes of the slice: x: 4 (x_hi: 2, x_lo: 2; x = x_hi * 2 + x_lo), y: 4, z: 8, core: 2. Of those that a mesh axis runs over, the one named last changes fastest.
Arguments:
- queries: bfloat16 [32768, 512], P(('dp', 'qrow', 'kcol')), parts along dimension 0, may hold values from -1.6953125 to 1.6953125
- keys: bfloat16 [32768, 128], P(('dp', 'qrow', 'kcol')), parts along dimension 0, may hold values from -1.6953125 to 1.6953125
- values: bfloat16 [32768, 128], P(('dp', 'qrow', 'kcol')), parts along dimension 0, may hold values from -0.5 to 0.5
- outputs: bfloat16 [32768, 512], P(('dp', 'qrow', 'kcol')), parts along dimension 0, may hold values from -0.59765625 to 0.59765625
- out_grad: bfloat16 [32768, 512], P(('dp', 'qrow', 'kcol')), parts along dimension 0, may hold values from -6 to 6
- log_norm: float32 [32768, 4], P(('dp', 'qrow', 'kcol')), parts along dimension 0
- positions: int32 [32768], P('dp'), parts along dimension 0, may hold values from 0 to 16383, as said below
Outputs:
- query_grad: bfloat16 [32768, 512], P(('dp', 'qrow', 'kcol')), parts along dimension 0
- key_grad: bfloat16 [32768, 128], P(('dp', 'qrow', 'kcol')), parts along dimension 0
- value_grad: bfloat16 [32768, 128], P(('dp', 'qrow', 'kcol')), parts along dimension 0
The draws below stay inside these ranges and needn't reach their ends.
There are 2 independent parts, one for each index of `dp`. The reference program is written for one: setup_inputs(seed, part) draws one part's arguments, and reference() takes and returns one part's arrays. A program takes and returns all parts, laid end to end along the dimension named above; each array names one. Nothing has to cross between parts.
Inputs may be any that keep to these rules, and one draw needn't show every extreme that they name: `positions`: each position 0 to 16383 appears once.
All inputs are finite; a program needn't handle non-finite values.
Results may differ from the reference program's by a relative error of at most 0.022.
Values may be sent and summed in bfloat16 or wider, within the bound.
No kernel may reach another device: no remote copies, remote signals or barrier semaphores. Data moves between devices by JAX's collectives and lax.ppermute only.
A program may use at most 64 MiB of HBM per device.

```python
import math
import jax
import jax.numpy as jnp
from jax import lax

HD = 128
HEADS = 4
TOK_DEV = 128
TOKENS = 16384
N_KCOL = 8


def token_positions(key):
    run_count = TOKENS // TOK_DEV
    jitter = jax.random.randint(jax.random.fold_in(key, 5), (run_count,), 0, max(run_count // 4, 2))
    ranked = (jnp.arange(run_count, dtype=jnp.int32) + jitter) * run_count + jnp.arange(run_count, dtype=jnp.int32)
    order = jnp.argsort(ranked, stable=True).astype(jnp.int32)
    slots = jnp.arange(TOKENS, dtype=jnp.int32)
    return (order[slots // TOK_DEV] * TOK_DEV + slots % TOK_DEV).astype(jnp.int32)


def draw_positions(key, part):
    return token_positions(key)


def draw_log_norm(key, part):
    placed = token_positions(key).astype(jnp.float32)
    key = jax.random.fold_in(key, 3)
    noise = jax.random.uniform(key, (TOKENS, HEADS), jnp.float32, 0.0, 1.0)
    return 0.5 * jnp.log(placed + 1.0)[:, None] + noise


def steps_of(stream_key, dims, cuts, low, largest):
    def one(position, blocks):
        heights = jax.random.uniform(jax.random.fold_in(jax.random.fold_in(stream_key, 6), position), (blocks,), jnp.float32, low / len(cuts), largest / len(cuts))
        return jnp.repeat(jnp.exp(heights), dims[position] // blocks).reshape((-1,) + (1,) * (len(dims) - position - 1))

    level = one(*cuts[0])
    for cut in cuts[1:]:
        level = level * one(*cut)
    return level


def bell_draw(stream_key, extent, scale, reach, split=(), kind=jnp.bfloat16):
    array = jax.random.normal(stream_key, extent, jnp.float32) * scale
    if len(split) > 0:
        array = steps_of(stream_key, extent, split, -0.22, 0.18) * array
    return jnp.clip(array, min=-reach, max=reach).astype(kind)


def setup_inputs(seed: int = 0, part: int = 0) -> dict:
    key_of = jax.random.split(jax.random.key(seed), 8)
    own_keys = jax.random.split(jax.random.fold_in(key_of[7], part), 8)
    return {
        "queries": jnp.clip(jax.random.uniform(own_keys[0], (TOKENS, HEADS * HD), jnp.float32, -1.6953125, 1.6953125) * steps_of(own_keys[0], (TOKENS, HEADS * HD), ((0, 128),), -0.4, 0.0), -1.6953125, 1.6953125).astype(jnp.bfloat16),
        "keys": jnp.clip(jax.random.uniform(own_keys[1], (TOKENS, HD), jnp.float32, -1.6953125, 1.6953125) * steps_of(own_keys[1], (TOKENS, HD), ((0, 128),), -0.4, 0.0), -1.6953125, 1.6953125).astype(jnp.bfloat16),
        "values": bell_draw(own_keys[2], (TOKENS, HD), 0.088, 0.5, ((0, 128),)),
        "outputs": bell_draw(own_keys[3], (TOKENS, HEADS * HD), 0.09, 0.59765625, ((0, 128),)),
        "out_grad": bell_draw(own_keys[4], (TOKENS, HEADS * HD), 1.0, 6.0, ((0, 128),)),
        "log_norm": draw_log_norm(jax.random.fold_in(jax.random.fold_in(key_of[7], part), 71), part),
        "positions": draw_positions(jax.random.fold_in(jax.random.fold_in(key_of[7], part), 71), part),
    }


def reference(queries, keys, values, outputs, out_grad, log_norm, positions):
    score_scale = 1.0 / math.sqrt(HD)
    block_rows = TOK_DEV * N_KCOL
    block_count = TOKENS // block_rows
    grad_heads = out_grad.astype(jnp.float32).reshape(TOKENS, HEADS, HD)
    row_delta = lax.optimization_barrier(jnp.sum(grad_heads * outputs.astype(jnp.float32).reshape(TOKENS, HEADS, HD), axis=-1))
    key_full = keys.astype(jnp.float32)
    value_full = values.astype(jnp.float32)
    query_heads = queries.astype(jnp.float32).reshape(TOKENS, HEADS, HD)

    def block_step(carry, block_index):
        key_total, value_total = carry
        first_row = (block_index * block_rows).astype(jnp.int32)
        query_block = lax.dynamic_slice_in_dim(query_heads, first_row, block_rows, 0)
        grad_block = lax.dynamic_slice_in_dim(grad_heads, first_row, block_rows, 0)
        norm_block = lax.dynamic_slice_in_dim(log_norm, first_row, block_rows, 0)
        delta_block = lax.dynamic_slice_in_dim(row_delta, first_row, block_rows, 0)
        pos_block = lax.dynamic_slice_in_dim(positions, first_row, block_rows, 0)
        scores = jnp.einsum('qhd,kd->hqk', query_block, key_full) * score_scale
        causal = pos_block[:, None] >= positions[None, :]
        probs = jnp.where(causal[None], jnp.exp(scores - norm_block.T[:, :, None]), jnp.float32(0.0))
        probs_low = probs.astype(jnp.bfloat16).astype(jnp.float32)
        prob_grad = jnp.einsum('qhd,kd->hqk', grad_block, value_full)
        score_grad = (probs * (prob_grad - delta_block.T[:, :, None]) * score_scale).astype(jnp.bfloat16).astype(jnp.float32)
        query_part = jnp.einsum('hqk,kd->qhd', score_grad, key_full).reshape(block_rows, HEADS * HD)
        key_total = key_total + jnp.einsum('hqk,qhd->kd', score_grad, query_block)
        value_total = value_total + jnp.einsum('hqk,qhd->kd', probs_low, grad_block)
        return ((key_total, value_total), query_part.astype(jnp.bfloat16))
    start_state = (jnp.zeros((TOKENS, HD), jnp.float32), jnp.zeros((TOKENS, HD), jnp.float32))
    totals, query_parts = lax.scan(block_step, start_state, jnp.arange(block_count, dtype=jnp.int32))
    query_grad = query_parts.reshape(TOKENS, HEADS * HD)
    return (query_grad, totals[0].astype(jnp.bfloat16), totals[1].astype(jnp.bfloat16))
```

```python
import functools
import math

import jax
import jax.numpy as jnp
from jax import lax
from jax.experimental import pallas as pl
from jax.experimental.pallas import tpu as pltpu
from jax.sharding import Mesh, PartitionSpec as P

F32 = jnp.float32
BF16 = jnp.bfloat16

HEADS = 4
HD = 128
TOK = 128
N_Z, N_CORE, N_XL, N_Y = 8, 2, 2, 4
ROWS = 2 * TOK + 16
N_QB = N_CORE * N_Y
N_KB = N_Z * N_XL
SCALE = 1.0 / math.sqrt(HD)
LOG2E = math.log2(math.e)
LN2 = math.log(2.0)
VMEM_LIMIT = 48 * 2**20

VMEM = pl.BlockSpec(memory_space=pltpu.VMEM)
SMEM = pl.BlockSpec(memory_space=pltpu.SMEM)


def split3(x):
    hi = x.astype(BF16)
    rest = x - hi.astype(F32)
    mid = rest.astype(BF16)
    low = (rest - mid.astype(F32)).astype(BF16)
    return [hi, mid, low]


def prep_kernel(q_ref, k_ref, v_ref, o_ref, g_ref, n_ref, qp_ref, kv_ref):
    qp_ref[0:TOK, :] = q_ref[...]
    qp_ref[TOK : 2 * TOK, :] = g_ref[...]
    deltas, norms = [], []
    for h in range(HEADS):
        cols = slice(h * HD, (h + 1) * HD)
        prod = g_ref[:, cols].astype(F32) * o_ref[:, cols].astype(F32)
        deltas.append(jnp.sum(prod.T, axis=0, keepdims=True))
        spread = jnp.broadcast_to(n_ref[:, h : h + 1] * LOG2E, (TOK, TOK))
        norms.append(spread.T[0:1, :])
    parts = split3(jnp.concatenate(norms, axis=1)) + split3(jnp.concatenate(deltas, axis=1))
    parts = [p.astype(F32) for p in parts] + [jnp.zeros((10, HEADS * TOK), F32)]
    qp_ref[2 * TOK : ROWS, :] = jnp.concatenate(parts, axis=0).astype(BF16)
    kv_ref[:, 0:HD] = (k_ref[...].astype(F32) * (SCALE * LOG2E)).astype(BF16)
    kv_ref[:, HD : 2 * HD] = v_ref[...]


def main_kernel(tk, where_ref, q0_ref, q1_ref, q2_ref, q3_ref, qs_ref, kv_ref, pos_ref,
                dqo_ref, dqs_ref, dkv_ref, kt_ref, kpos_ref, dqt_ref, qst_ref, gst_ref, row_ref):
    z, core, xl, y = where_ref[0], where_ref[1], where_ref[2], where_ref[3]
    for j in range(N_KB):
        rows = slice(j * TOK, (j + 1) * TOK)
        kt_ref[:, rows] = kv_ref[rows, 0:HD].T
        block = (j // N_XL) * 16 + core * 8 + (j % N_XL) * 4 + y
        line = pos_ref[pl.ds(block, 1), :].astype(F32)
        kpos_ref[rows, :] = jnp.broadcast_to(line, (TOK, TOK)).T
    for b in range(N_QB):
        d = b % N_Y
        if b < N_Y:
            src, base = (q0_ref, q1_ref, q2_ref, q3_ref)[d], 0
        else:
            src, base = qs_ref, d * ROWS
        for h in range(HEADS):
            cols = slice(h * HD, (h + 1) * HD)
            out = slice(h * TOK, (h + 1) * TOK)
            qst_ref[b, out, :] = src[base : base + TOK, cols]
            gst_ref[b, out, :] = src[base + TOK : base + 2 * TOK, cols]
        aux = src[base + 2 * TOK : base + ROWS, :].astype(F32)
        row_ref[b, 0:1, :] = (aux[2:3] + aux[1:2]) + aux[0:1]
        row_ref[b, 1:2, :] = (aux[5:6] + aux[4:5]) + aux[3:4]
        owner = core if b < N_Y else 1 - core
        block = z * 16 + owner * 8 + xl * 4 + lax.rem(y + d, N_Y)
        line = pos_ref[pl.ds(block, 1), :].astype(F32)
        row_ref[b, 2:3, :] = jnp.concatenate([line] * HEADS, axis=1)

    def key_step(ki, _):
        ks = pl.ds(pl.multiple_of(ki * tk, tk), tk)
        k = kv_ref[ks, 0:HD]
        v = kv_ref[ks, HD : 2 * HD]
        kt = kt_ref[:, ks]
        kpos = kpos_ref[ks, :]

        def query_step(b, carry):
            dk, dv = carry
            q = qst_ref[b]
            g = gst_ref[b]
            s = lax.dot_general(k, q, (((1,), (1,)), ((), ())), preferred_element_type=F32)
            dp = lax.dot_general(v, g, (((1,), (1,)), ((), ())), preferred_element_type=F32)
            keep = row_ref[b, 2:3, 0:TOK] >= kpos
            keep = jnp.concatenate([keep] * HEADS, axis=1)
            p = jnp.where(keep, jnp.exp2(s - row_ref[b, 0:1, :]), 0.0)
            ds = (p * (dp - row_ref[b, 1:2, :])).astype(BF16)
            dv = dv + jnp.dot(p.astype(BF16), g, preferred_element_type=F32)
            dk = dk + jnp.dot(ds, q, preferred_element_type=F32)
            dq = jnp.dot(kt, ds, preferred_element_type=F32)
            dqt_ref[b] = jnp.where(ki == 0, dq, dqt_ref[b] + dq)
            return dk, dv

        zero = jnp.zeros((tk, HD), F32)
        dk, dv = lax.fori_loop(0, N_QB, query_step, (zero, zero), unroll=4)
        dkv_ref[ks, 0:HD] = (dk * SCALE).astype(BF16)
        dkv_ref[ks, HD : 2 * HD] = dv.astype(BF16)
        return 0

    lax.fori_loop(0, N_KB * TOK // tk, key_step, 0)
    for b in range(N_QB):
        out = dqo_ref if b < N_Y else dqs_ref
        d = b % N_Y
        for h in range(HEADS):
            blk = dqt_ref[b, :, h * TOK : (h + 1) * TOK] * LN2
            out[d * TOK : (d + 1) * TOK, h * HD : (h + 1) * HD] = blk.T.astype(BF16)


def shift_y(x, d):
    return lax.ppermute(x, "y", [(i, (i - d) % N_Y) for i in range(N_Y)])


def swap_core(x):
    return lax.ppermute(x, "core", [(0, 1), (1, 0)])


def shards(queries, keys, values, outputs, out_grad, log_norm, positions):
    params = pltpu.CompilerParams(vmem_limit_bytes=VMEM_LIMIT)
    where = jnp.stack([lax.axis_index(a) for a in ("z", "core", "xl", "y")]).astype(jnp.int32)
    q_pay, kv_pay = pl.pallas_call(
        prep_kernel,
        in_specs=[VMEM] * 6,
        out_specs=[VMEM] * 2,
        out_shape=[
            jax.ShapeDtypeStruct((ROWS, HEADS * HD), BF16),
            jax.ShapeDtypeStruct((TOK, 2 * HD), BF16),
        ],
        compiler_params=params,
        name="prep",
    )(queries, keys, values, outputs, out_grad, log_norm)
    q1 = shift_y(q_pay, 1)
    q3 = shift_y(q_pay, 3)
    q2 = shift_y(q_pay, 2)
    kv_send = jnp.broadcast_to(kv_pay[None], (N_KB, TOK, 2 * HD)).reshape(N_KB * TOK, 2 * HD)
    kv_all = lax.all_to_all(kv_send, ("z", "xl"), 0, 0, tiled=True)
    q_other = swap_core(jnp.concatenate([q_pay, q1, q2, q3], axis=0))
    dq_own, dq_swap, dkv = pl.pallas_call(
        functools.partial(main_kernel, 512),
        in_specs=[SMEM] + [VMEM] * 7,
        out_specs=[VMEM] * 3,
        out_shape=[
            jax.ShapeDtypeStruct((N_Y * TOK, HEADS * HD), BF16),
            jax.ShapeDtypeStruct((N_Y * TOK, HEADS * HD), BF16),
            jax.ShapeDtypeStruct((N_KB * TOK, 2 * HD), BF16),
        ],
        scratch_shapes=[
            pltpu.VMEM((HD, N_KB * TOK), BF16),
            pltpu.VMEM((N_KB * TOK, TOK), F32),
            pltpu.VMEM((N_QB, HD, HEADS * TOK), F32),
            pltpu.VMEM((N_QB, HEADS * TOK, HD), BF16),
            pltpu.VMEM((N_QB, HEADS * TOK, HD), BF16),
            pltpu.VMEM((N_QB, 8, HEADS * TOK), F32),
        ],
        compiler_params=params,
        cost_estimate=pl.CostEstimate(
            flops=10 * HEADS * HD * N_QB * N_KB * TOK * TOK,
            bytes_accessed=8 * 2**20,
            transcendentals=HEADS * N_QB * N_KB * TOK * TOK,
        ),
        name="attend",
    )(where, q_pay, q1, q2, q3, q_other, kv_all, positions.reshape(-1, TOK))
    dq_sum = dq_own.astype(F32) + swap_core(dq_swap).astype(F32)
    dq_low = dq_sum.astype(BF16).reshape(N_Y, TOK, HEADS * HD)
    got = [shift_y(dq_low[d], N_Y - d) for d in (1, 3, 2)]
    kv_got = lax.all_to_all(dkv, ("z", "xl"), 0, 0, tiled=True)
    kv_sum = jnp.sum(kv_got.reshape(N_KB, TOK, 2 * HD).astype(F32), axis=0)
    dq = dq_sum[0:TOK]
    for part in got:
        dq = dq + part.astype(F32)
    return (
        dq.astype(BF16),
        kv_sum[:, 0:HD].astype(BF16),
        kv_sum[:, HD : 2 * HD].astype(BF16),
    )


def solution(mesh):
    dp = mesh.devices.shape[0]
    grid = Mesh(
        mesh.devices.reshape(dp, N_Z, N_CORE, N_XL, N_Y), ("dp", "z", "core", "xl", "y")
    )
    rows = P(("dp", "z", "core", "xl", "y"), None)
    return jax.shard_map(
        shards,
        mesh=grid,
        in_specs=(rows,) * 6 + (P("dp"),),
        out_specs=(rows,) * 3,
        check_vma=False,
    )
```

```python
import functools
import math

import jax
import jax.numpy as jnp
from jax import lax
from jax.experimental import pallas as pl
from jax.experimental.pallas import tpu as pltpu
from jax.sharding import Mesh, PartitionSpec as P

F32 = jnp.float32
BF16 = jnp.bfloat16

HEADS = 4
HD = 128
TOK = 128
N_Z, N_CORE, N_XL, N_Y = 8, 2, 2, 4
ROWS = 2 * TOK + 16
N_QB = N_CORE * N_Y
SCALE = 1.0 / math.sqrt(HD)
LOG2E = math.log2(math.e)
LN2 = math.log(2.0)
VMEM_LIMIT = 60 * 2**20

VMEM = pl.BlockSpec(memory_space=pltpu.VMEM)


def split3(x):
    hi = x.astype(BF16)
    rest = x - hi.astype(F32)
    mid = rest.astype(BF16)
    low = (rest - mid.astype(F32)).astype(BF16)
    return [hi, mid, low]


def prep_kernel(q_ref, k_ref, v_ref, o_ref, g_ref, n_ref, qp_ref, kv_ref):
    qp_ref[0:TOK, :] = q_ref[...]
    qp_ref[TOK : 2 * TOK, :] = g_ref[...]
    key = (k_ref[...].astype(F32) * (SCALE * LOG2E)).astype(BF16)
    for j in range(N_Z):
        kv_ref[j * TOK : (j + 1) * TOK, 0:HD] = key
        kv_ref[j * TOK : (j + 1) * TOK, HD : 2 * HD] = v_ref[...]
    deltas, norms = [], []
    for h in range(HEADS):
        cols = slice(h * HD, (h + 1) * HD)
        prod = g_ref[:, cols].astype(F32) * o_ref[:, cols].astype(F32)
        deltas.append(jnp.sum(prod.T, axis=0, keepdims=True))
        norms.append(n_ref[h : h + 1, :] * LOG2E)
    parts = split3(jnp.concatenate(norms, axis=1)) + split3(jnp.concatenate(deltas, axis=1))
    parts = [p.astype(F32) for p in parts] + [jnp.zeros((10, HEADS * TOK), F32)]
    qp_ref[2 * TOK : ROWS, :] = jnp.concatenate(parts, axis=0).astype(BF16)


def main_kernel(tk, is_last, *refs):
    own_refs, other_refs, kv_ref, pos_ref = refs[0:4], refs[4:8], refs[8], refs[9]
    refs = refs[10:]
    if is_last:
        dq_in_ref, refs = refs[0], refs[1:]
    if is_last:
        dqo_ref, dqs_ref, dkv_ref, kt_ref, kpos_ref, dqt_ref, qst_ref, gst_ref, row_ref = refs
    else:
        dqt_ref, dkv_ref, kt_ref, kpos_ref, qst_ref, gst_ref, row_ref = refs
    z, core, xl, y = (lax.axis_index(a) for a in ("z", "core", "xl", "y"))
    column = 1 - xl if is_last else xl
    for j in range(N_Z):
        rows = slice(j * TOK, (j + 1) * TOK)
        kt_ref[:, rows] = kv_ref[rows, 0:HD].T
        block = j * 16 + core * 8 + column * 4 + y
        line = pos_ref[pl.ds(block, 1), :].astype(F32)
        kpos_ref[rows, :] = jnp.broadcast_to(line, (TOK, TOK)).T
    for b in range(N_QB):
        d = b % N_Y
        src = own_refs[d] if b < N_Y else other_refs[d]
        for h in range(HEADS):
            cols = slice(h * HD, (h + 1) * HD)
            out = slice(h * TOK, (h + 1) * TOK)
            qst_ref[b, out, :] = src[0:TOK, cols]
            gst_ref[b, out, :] = src[TOK : 2 * TOK, cols]
        aux = src[2 * TOK : ROWS, :].astype(F32)
        row_ref[b, 0:1, :] = (aux[2:3] + aux[1:2]) + aux[0:1]
        row_ref[b, 1:2, :] = (aux[5:6] + aux[4:5]) + aux[3:4]
        owner = core if b < N_Y else 1 - core
        block = z * 16 + owner * 8 + xl * 4 + lax.rem(y + d, N_Y)
        line = pos_ref[pl.ds(block, 1), :].astype(F32)
        row_ref[b, 2:3, :] = jnp.concatenate([line] * HEADS, axis=1)

    def key_step(ki, _):
        ks = pl.ds(pl.multiple_of(ki * tk, tk), tk)
        k = kv_ref[ks, 0:HD]
        v = kv_ref[ks, HD : 2 * HD]
        kt = kt_ref[:, ks]
        kpos = kpos_ref[ks, :]

        def query_step(b, carry):
            dk, dv = carry
            q = qst_ref[b]
            g = gst_ref[b]
            s = lax.dot_general(k, q, (((1,), (1,)), ((), ())), preferred_element_type=F32)
            dp = lax.dot_general(v, g, (((1,), (1,)), ((), ())), preferred_element_type=F32)
            keep = row_ref[b, 2:3, 0:TOK] >= kpos
            keep = jnp.concatenate([keep] * HEADS, axis=1)
            p = jnp.where(keep, jnp.exp2(s - row_ref[b, 0:1, :]), 0.0)
            ds = (p * (dp - row_ref[b, 1:2, :])).astype(BF16)
            dv = dv + jnp.dot(p.astype(BF16), g, preferred_element_type=F32)
            dk = dk + jnp.dot(ds, q, preferred_element_type=F32)
            dq = jnp.dot(kt, ds, preferred_element_type=F32)
            if is_last:
                dqt_ref[b] = jnp.where(ki == 0, dq_in_ref[b], dqt_ref[b]) + dq
            else:
                dqt_ref[b] = jnp.where(ki == 0, dq, dqt_ref[b] + dq)
            return dk, dv

        zero = jnp.zeros((tk, HD), F32)
        dk, dv = lax.fori_loop(0, N_QB, query_step, (zero, zero), unroll=4)
        dkv_ref[ks, 0:HD] = (dk * SCALE).astype(BF16)
        dkv_ref[ks, HD : 2 * HD] = dv.astype(BF16)
        return 0

    lax.fori_loop(0, N_Z * TOK // tk, key_step, 0)
    if is_last:
        for b in range(N_QB):
            out = dqo_ref if b < N_Y else dqs_ref
            d = b % N_Y
            for h in range(HEADS):
                blk = dqt_ref[b, :, h * TOK : (h + 1) * TOK] * LN2
                out[d * TOK : (d + 1) * TOK, h * HD : (h + 1) * HD] = blk.T.astype(BF16)


def whole(*shape):
    return pl.BlockSpec(shape, lambda i: (0,) * len(shape), pipeline_mode=pl.Buffered(1))


def whole_of(x):
    return whole(*x.shape)


PARAMS = pltpu.CompilerParams(vmem_limit_bytes=VMEM_LIMIT)


def attend(own, other, kv, pos, dq_in):
    is_last = dq_in is not None
    keys = N_Z * TOK
    dqt = (N_QB, HD, HEADS * TOK)
    dkv_shape = jax.ShapeDtypeStruct((keys, 2 * HD), BF16)
    if is_last:
        half = jax.ShapeDtypeStruct((N_Y * TOK, HEADS * HD), BF16)
        out_shape = [half, half, dkv_shape]
    else:
        out_shape = [jax.ShapeDtypeStruct(dqt, F32), dkv_shape]
    scratch = [pltpu.VMEM((HD, keys), BF16), pltpu.VMEM((keys, TOK), F32)]
    if is_last:
        scratch.append(pltpu.VMEM(dqt, F32))
    scratch += [
        pltpu.VMEM((N_QB, HEADS * TOK, HD), BF16),
        pltpu.VMEM((N_QB, HEADS * TOK, HD), BF16),
        pltpu.VMEM((N_QB, 8, HEADS * TOK), F32),
    ]
    args = [*own, *other, kv, pos] + ([dq_in] if is_last else [])
    return pl.pallas_call(
        functools.partial(main_kernel, 512, is_last),
        in_specs=[VMEM] * len(args),
        out_specs=[VMEM] * len(out_shape),
        out_shape=out_shape,
        scratch_shapes=scratch,
        compiler_params=pltpu.CompilerParams(vmem_limit_bytes=28 * 2**20),
        cost_estimate=pl.CostEstimate(
            flops=10 * HEADS * HD * N_QB * TOK * keys,
            bytes_accessed=8 * 2**20,
            transcendentals=HEADS * N_QB * TOK * keys,
        ),
        name="attend",
    )(*args)


def shift_y(x, d):
    return lax.ppermute(x, "y", [(i, (i - d) % N_Y) for i in range(N_Y)])


def swap(x, axis):
    return lax.ppermute(x, axis, [(0, 1), (1, 0)])


def shards(queries, keys, values, outputs, out_grad, log_norm, positions):
    args = (queries, keys, values, outputs, out_grad, log_norm.T)
    pays = [
        jax.ShapeDtypeStruct((ROWS, HEADS * HD), BF16),
        jax.ShapeDtypeStruct((N_Z * TOK, 2 * HD), BF16),
    ]
    q_pay, kv_send = pl.pallas_call(
        prep_kernel,
        grid=(1,),
        in_specs=[whole_of(x) for x in args],
        out_specs=[whole_of(x) for x in pays],
        out_shape=pays,
        compiler_params=PARAMS,
        name="prep",
    )(*args)
    pos = positions.reshape(-1, TOK)
    own = [q_pay] + [None] * 3
    for d in (1, 3, 2):
        own[d] = shift_y(q_pay, d)
    kv = lax.all_to_all(kv_send, "z", 0, 0, tiled=True)
    own, kv = lax.optimization_barrier((own, kv))
    other = [swap(x, "core") for x in own]
    kv_far = swap(kv, "xl")
    dqt, dkv = attend(own, other, kv, pos, None)
    dkv_got = swap(dkv, "xl")
    dq_own, dq_swap, dkv_far = attend(own, other, kv_far, pos, dqt)
    dq_sum = dq_own.astype(F32) + swap(dq_swap, "core").astype(F32)
    dq_low = dq_sum.astype(BF16).reshape(N_Y, TOK, HEADS * HD)
    kv_sum = (dkv_far.astype(F32) + dkv_got.astype(F32)).astype(BF16)
    dq_got = [shift_y(dq_low[d], N_Y - d) for d in (1, 3, 2)]
    kv_got = lax.all_to_all(kv_sum, "z", 0, 0, tiled=True)
    dkv = jnp.sum(kv_got.reshape(N_Z, TOK, 2 * HD).astype(F32), axis=0)
    dkv = swap(dkv.astype(BF16), "xl")
    dq = dq_sum[0:TOK]
    for part in dq_got:
        dq = dq + part.astype(F32)
    return dq.astype(BF16), dkv[:, 0:HD], dkv[:, HD : 2 * HD]


def solution(mesh):
    dp = mesh.devices.shape[0]
    grid = Mesh(
        mesh.devices.reshape(dp, N_Z, N_CORE, N_XL, N_Y), ("dp", "z", "core", "xl", "y")
    )
    rows = P(("dp", "z", "core", "xl", "y"), None)
    return jax.shard_map(
        shards,
        mesh=grid,
        in_specs=(rows,) * 6 + (P("dp"),),
        out_specs=(rows,) * 3,
        check_vma=False,
    )
```

```python
import functools
import math

import jax
import jax.numpy as jnp
from jax import lax
from jax.experimental import pallas as pl
from jax.experimental.pallas import tpu as pltpu
from jax.sharding import Mesh, PartitionSpec as P

F32 = jnp.float32
BF16 = jnp.bfloat16

HEADS = 4
HD = 128
TOK = 128
N_Z, N_CORE, N_XL, N_Y = 8, 2, 2, 4
ROWS = 2 * TOK + 16
N_QB = N_CORE * N_Y
TILE = 512
STEP = 4
SCALE = 1.0 / math.sqrt(HD)
LOG2E = math.log2(math.e)
LN2 = math.log(2.0)
VMEM_LIMIT = 60 * 2**20
LOCAL_LIMIT = 24 * 2**20

VMEM = pl.BlockSpec(memory_space=pltpu.VMEM)


def split3(x):
    hi = x.astype(BF16)
    rest = x - hi.astype(F32)
    mid = rest.astype(BF16)
    low = (rest - mid.astype(F32)).astype(BF16)
    return [hi, mid, low]


def prep_kernel(q_ref, k_ref, v_ref, o_ref, g_ref, n_ref, qp_ref, kv_ref):
    qp_ref[0:TOK, :] = q_ref[...]
    qp_ref[TOK : 2 * TOK, :] = g_ref[...]
    key = (k_ref[...].astype(F32) * (SCALE * LOG2E)).astype(BF16)
    for j in range(N_Z):
        kv_ref[j * TOK : (j + 1) * TOK, 0:HD] = key
        kv_ref[j * TOK : (j + 1) * TOK, HD : 2 * HD] = v_ref[...]
    deltas, norms = [], []
    for h in range(HEADS):
        cols = slice(h * HD, (h + 1) * HD)
        prod = g_ref[:, cols].astype(F32) * o_ref[:, cols].astype(F32)
        deltas.append(jnp.sum(prod.T, axis=0, keepdims=True))
        norms.append(n_ref[h : h + 1, :] * LOG2E)
    parts = split3(jnp.concatenate(norms, axis=1)) + split3(jnp.concatenate(deltas, axis=1))
    parts = [p.astype(F32) for p in parts] + [jnp.zeros((10, HEADS * TOK), F32)]
    qp_ref[2 * TOK : ROWS, :] = jnp.concatenate(parts, axis=0).astype(BF16)


def keep_kernel(pay_ref, pos_ref, keep_ref, line_ref, near_ref, far_ref):
    keep_ref[...] = pay_ref[...]
    z, core, xl, y = (lax.axis_index(a) for a in ("z", "core", "xl", "y"))
    for b in range(N_QB):
        owner = core if b < N_Y else 1 - core
        block = z * 16 + owner * 8 + xl * 4 + lax.rem(y + b % N_Y, N_Y)
        line_ref[b : b + 1, :] = pos_ref[pl.ds(block, 1), :].astype(F32)
    for j in range(N_Z):
        for column, out in ((xl, near_ref), (1 - xl, far_ref)):
            block = j * 16 + core * 8 + column * 4 + y
            line = pos_ref[pl.ds(block, 1), :].astype(F32)
            out[j * TOK : (j + 1) * TOK, :] = jnp.broadcast_to(line, (TOK, TOK)).T


def stack_kernel(*refs):
    own_refs, other_refs, line_ref = refs[0:4], refs[4:8], refs[8]
    q_ref, g_ref, row_ref = refs[9:]
    for b in range(N_QB):
        d = b % N_Y
        src = own_refs[d] if b < N_Y else other_refs[d]
        for h in range(HEADS):
            cols = slice(h * HD, (h + 1) * HD)
            out = slice((b * HEADS + h) * TOK, (b * HEADS + h + 1) * TOK)
            q_ref[out, :] = src[0:TOK, cols]
            g_ref[out, :] = src[TOK : 2 * TOK, cols]
        aux = src[2 * TOK : ROWS, :].astype(F32)
        cols = slice(b * HEADS * TOK, (b + 1) * HEADS * TOK)
        row_ref[0:1, cols] = (aux[2:3] + aux[1:2]) + aux[0:1]
        row_ref[1:2, cols] = (aux[5:6] + aux[4:5]) + aux[3:4]
        row_ref[2:3, cols] = jnp.concatenate([line_ref[b : b + 1, :]] * HEADS, axis=1)


def slot_of(block):
    d = lax.rem(block - lax.axis_index("z") + N_Z, N_Z)
    low, high = lax.rem(d, 4), d // 4
    flip = jnp.where(low == 3, 1, jnp.where(low == 2, lax.axis_index("core"), 0))
    return low * 2 + lax.rem(high + flip, 2)


def main_kernel(is_last, q_ref, g_ref, row_ref, kv_ref, kpos_ref, *refs):
    if is_last:
        dq_in_ref, dqo_ref, dqs_ref, dkv_ref, kt_ref, dqt_ref = refs
    else:
        dqt_ref, dkv_ref, kt_ref = refs
    for j in range(N_Z):
        rows = slice(j * TOK, (j + 1) * TOK)
        kt_ref[:, rows] = kv_ref[rows, 0:HD].T
    for first in range(0, N_Z * TOK, TILE):
        ks = slice(first, first + TILE)
        k = kv_ref[ks, 0:HD]
        v = kv_ref[ks, HD : 2 * HD]
        kt = kt_ref[:, ks]
        dk = jnp.zeros((TILE, HD), F32)
        dv = jnp.zeros((TILE, HD), F32)
        for b in range(0, N_QB, STEP):
            rs = slice(b * HEADS * TOK, (b + STEP) * HEADS * TOK)
            q = q_ref[rs, :]
            g = g_ref[rs, :]
            s = lax.dot_general(k, q, (((1,), (1,)), ((), ())), preferred_element_type=F32)
            dp = lax.dot_general(v, g, (((1,), (1,)), ((), ())), preferred_element_type=F32)
            keep = []
            for i in range(b, b + STEP):
                at = i * HEADS * TOK
                keep += [row_ref[2:3, at : at + TOK] >= kpos_ref[ks, :]] * HEADS
            p = jnp.where(jnp.concatenate(keep, axis=1), jnp.exp2(s - row_ref[0:1, rs]), 0.0)
            ds = (p * (dp - row_ref[1:2, rs])).astype(BF16)
            dv = dv + jnp.dot(p.astype(BF16), g, preferred_element_type=F32)
            dk = dk + jnp.dot(ds, q, preferred_element_type=F32)
            dq = jnp.dot(kt, ds, preferred_element_type=F32)
            if first > 0:
                dqt_ref[:, rs] += dq
            elif is_last:
                dqt_ref[:, rs] = dq_in_ref[:, rs] + dq
            else:
                dqt_ref[:, rs] = dq
        for i in range(TILE // TOK):
            at = slice(i * TOK, (i + 1) * TOK)
            out = pl.ds(pl.multiple_of(slot_of(first // TOK + i) * TOK, TOK), TOK)
            dkv_ref[out, 0:HD] = (dk[at] * SCALE).astype(BF16)
            dkv_ref[out, HD : 2 * HD] = dv[at].astype(BF16)
    if is_last:
        for b in range(N_QB):
            out = dqo_ref if b < N_Y else dqs_ref
            d = b % N_Y
            for h in range(HEADS):
                at = (b * HEADS + h) * TOK
                blk = dqt_ref[:, at : at + TOK] * LN2
                out[d * TOK : (d + 1) * TOK, h * HD : (h + 1) * HD] = blk.T.astype(BF16)


def whole(*shape):
    return pl.BlockSpec(shape, lambda i: (0,) * len(shape), pipeline_mode=pl.Buffered(1))


def whole_of(x):
    return whole(*x.shape)


PARAMS = pltpu.CompilerParams(vmem_limit_bytes=VMEM_LIMIT)


def plain_call(kernel, out_shape, args):
    return pl.pallas_call(
        kernel,
        in_specs=[VMEM] * len(args),
        out_specs=[VMEM] * len(out_shape),
        out_shape=out_shape,
        compiler_params=pltpu.CompilerParams(vmem_limit_bytes=LOCAL_LIMIT),
        name=kernel.__name__,
    )(*args)


def keep(q_pay, pos):
    keys = N_Z * TOK
    out_shape = [
        jax.ShapeDtypeStruct((ROWS, HEADS * HD), BF16),
        jax.ShapeDtypeStruct((N_QB, TOK), F32),
        jax.ShapeDtypeStruct((keys, TOK), F32),
        jax.ShapeDtypeStruct((keys, TOK), F32),
    ]
    return plain_call(keep_kernel, out_shape, (q_pay, pos))


def stack(own, other, line):
    rows = N_QB * HEADS * TOK
    out_shape = [
        jax.ShapeDtypeStruct((rows, HD), BF16),
        jax.ShapeDtypeStruct((rows, HD), BF16),
        jax.ShapeDtypeStruct((8, rows), F32),
    ]
    return plain_call(stack_kernel, out_shape, (*own, *other, line))


def attend(q, g, row, kv, kpos, dq_in):
    is_last = dq_in is not None
    keys = N_Z * TOK
    rows = N_QB * HEADS * TOK
    dqt = (HD, rows)
    dkv_shape = jax.ShapeDtypeStruct((keys, 2 * HD), BF16)
    scratch = [pltpu.VMEM((HD, keys), BF16)]
    if is_last:
        half = jax.ShapeDtypeStruct((N_Y * TOK, HEADS * HD), BF16)
        out_shape = [half, half, dkv_shape]
        scratch.append(pltpu.VMEM(dqt, F32))
    else:
        out_shape = [jax.ShapeDtypeStruct(dqt, F32), dkv_shape]
    args = [q, g, row, kv, kpos] + ([dq_in] if is_last else [])
    return pl.pallas_call(
        functools.partial(main_kernel, is_last),
        in_specs=[VMEM] * len(args),
        out_specs=[VMEM] * len(out_shape),
        out_shape=out_shape,
        scratch_shapes=scratch,
        compiler_params=pltpu.CompilerParams(vmem_limit_bytes=LOCAL_LIMIT),
        cost_estimate=pl.CostEstimate(
            flops=10 * HD * rows * keys, bytes_accessed=8 * 2**20, transcendentals=rows * keys
        ),
        name="attend",
    )(*args)


def shift_y(x, d):
    return lax.ppermute(x, "y", [(i, (i - d) % N_Y) for i in range(N_Y)])


def swap(x, axis):
    return lax.ppermute(x, axis, [(0, 1), (1, 0)])


def finish_kernel(own_ref, *refs):
    total = own_ref[...]
    for ref in refs[:-1]:
        total = total + ref[...].astype(F32)
    refs[-1][...] = total.astype(BF16)


def finish(own, parts):
    return pl.pallas_call(
        finish_kernel,
        in_specs=[VMEM] * (1 + len(parts)),
        out_specs=VMEM,
        out_shape=jax.ShapeDtypeStruct(own.shape, BF16),
        compiler_params=pltpu.CompilerParams(vmem_limit_bytes=LOCAL_LIMIT),
        cost_estimate=pl.CostEstimate(flops=10**10, bytes_accessed=2**20, transcendentals=0),
        name="finish",
    )(own, *parts)


def move_z(x, by0, by1):
    pairs = [
        (z * N_CORE + c, (z + by) % N_Z * N_CORE + c)
        for z in range(N_Z)
        for c, by in ((0, by0), (1, by1))
    ]
    return lax.ppermute(x, ("z", "core"), pairs)


def cross(x):
    flat = lambda z, core, xl: (z * N_CORE + core) * N_XL + xl
    pairs = [
        (flat(z, c, xl), flat((z + 4) % N_Z, c, 1 - xl))
        for z in range(N_Z)
        for c in range(N_CORE)
        for xl in range(N_XL)
    ]
    return lax.ppermute(x, ("z", "core", "xl"), pairs)


def shards(queries, keys, values, outputs, out_grad, log_norm, positions):
    args = (queries, keys, values, outputs, out_grad, log_norm.T)
    pays = [
        jax.ShapeDtypeStruct((ROWS, HEADS * HD), BF16),
        jax.ShapeDtypeStruct((N_Z * TOK, 2 * HD), BF16),
    ]
    q_pay, kv_send = pl.pallas_call(
        prep_kernel,
        grid=(1,),
        in_specs=[whole_of(x) for x in args],
        out_specs=[whole_of(x) for x in pays],
        out_shape=pays,
        compiler_params=PARAMS,
        name="prep",
    )(*args)
    pos = positions.reshape(-1, TOK)
    own = [q_pay] + [None] * 3
    for d in (1, 3, 2):
        own[d] = shift_y(q_pay, d)
    kv = lax.all_to_all(kv_send, "z", 0, 0, tiled=True)
    mine, line, near, far = keep(q_pay, pos)
    own[3], mine, line, near, far = lax.optimization_barrier((own[3], mine, line, near, far))
    other = [swap(x, "core") for x in own]
    own[0] = mine
    kv_far = swap(kv, "xl")
    q, g, row = stack(own, other, line)
    dqt, dkv = attend(q, g, row, kv, near, None)
    dkv_got = swap(dkv, "xl")
    dq_own, dq_swap, dkv_far = attend(q, g, row, kv_far, far, dqt)
    dq_sum = dq_own.astype(F32) + swap(dq_swap, "core").astype(F32)
    dq_low = dq_sum.astype(BF16).reshape(N_Y, TOK, HEADS * HD)
    dq_got = [shift_y(dq_low[d], N_Y - d) for d in (1, 3, 2)]
    kv_sum = (dkv_far.astype(F32) + dkv_got.astype(F32)).astype(BF16).reshape(4, 2 * TOK, 2 * HD)
    pair = kv_sum[0].astype(F32)
    for part in (move_z(kv_sum[1], 1, 1), move_z(kv_sum[3], -1, -1), move_z(kv_sum[2], 2, -2)):
        pair = pair + part.astype(F32)
    pair = pair.astype(BF16)
    pair, dq_got = lax.optimization_barrier((pair, dq_got))
    dkv = swap(pair[0:TOK], "xl").astype(F32) + cross(pair[TOK : 2 * TOK]).astype(F32)
    dkv = dkv.astype(BF16)
    dq = finish(dq_sum[0:TOK], dq_got)
    return dq, dkv[:, 0:HD], dkv[:, HD : 2 * HD]


def solution(mesh):
    dp = mesh.devices.shape[0]
    grid = Mesh(
        mesh.devices.reshape(dp, N_Z, N_CORE, N_XL, N_Y), ("dp", "z", "core", "xl", "y")
    )
    rows = P(("dp", "z", "core", "xl", "y"), None)
    return jax.shard_map(
        shards,
        mesh=grid,
        in_specs=(rows,) * 6 + (P("dp"),),
        out_specs=(rows,) * 3,
        check_vma=False,
    )
```

```python
import functools
import math

import jax
import jax.numpy as jnp
from jax import lax
from jax.experimental import pallas as pl
from jax.experimental.pallas import tpu as pltpu
from jax.sharding import Mesh, PartitionSpec as P

F32 = jnp.float32
BF16 = jnp.bfloat16

HEADS = 4
HD = 128
TOK = 128
N_Z, N_CORE, N_XL, N_Y = 8, 2, 2, 4
ROWS = 2 * TOK + 16
N_QB = N_CORE * N_Y
TILE = 512
STEP = 4
SCALE = 1.0 / math.sqrt(HD)
LOG2E = math.log2(math.e)
LN2 = math.log(2.0)
VMEM_LIMIT = 60 * 2**20
LOCAL_LIMIT = 24 * 2**20

VMEM = pl.BlockSpec(memory_space=pltpu.VMEM)


def split3(x):
    hi = x.astype(BF16)
    rest = x - hi.astype(F32)
    mid = rest.astype(BF16)
    low = (rest - mid.astype(F32)).astype(BF16)
    return [hi, mid, low]


def prep_kernel(q_ref, k_ref, v_ref, o_ref, g_ref, n_ref, qp_ref, kv_ref):
    qp_ref[0:TOK, :] = q_ref[...]
    qp_ref[TOK : 2 * TOK, :] = g_ref[...]
    key = (k_ref[...].astype(F32) * (SCALE * LOG2E)).astype(BF16)
    for j in range(N_Z):
        kv_ref[j * TOK : (j + 1) * TOK, 0:HD] = key
        kv_ref[j * TOK : (j + 1) * TOK, HD : 2 * HD] = v_ref[...]
    deltas, norms = [], []
    for h in range(HEADS):
        cols = slice(h * HD, (h + 1) * HD)
        prod = g_ref[:, cols].astype(F32) * o_ref[:, cols].astype(F32)
        deltas.append(jnp.sum(prod.T, axis=0, keepdims=True))
        norms.append(n_ref[h : h + 1, :] * LOG2E)
    parts = split3(jnp.concatenate(norms, axis=1)) + split3(jnp.concatenate(deltas, axis=1))
    parts = [p.astype(F32) for p in parts] + [jnp.zeros((10, HEADS * TOK), F32)]
    qp_ref[2 * TOK : ROWS, :] = jnp.concatenate(parts, axis=0).astype(BF16)


def keep_kernel(pay_ref, pos_ref, keep_ref, line_ref, near_ref, far_ref):
    keep_ref[...] = pay_ref[...]
    z, core, xl, y = (lax.axis_index(a) for a in ("z", "core", "xl", "y"))
    for b in range(N_QB):
        owner = core if b < N_Y else 1 - core
        block = z * 16 + owner * 8 + xl * 4 + lax.rem(y + b % N_Y, N_Y)
        line_ref[b : b + 1, :] = pos_ref[pl.ds(block, 1), :].astype(F32)
    for j in range(N_Z):
        for column, out in ((xl, near_ref), (1 - xl, far_ref)):
            block = j * 16 + core * 8 + column * 4 + y
            line = pos_ref[pl.ds(block, 1), :].astype(F32)
            out[j * TOK : (j + 1) * TOK, :] = jnp.broadcast_to(line, (TOK, TOK)).T


def stack_kernel(*refs):
    own_refs, other_refs, line_ref = refs[0:4], refs[4:8], refs[8]
    q_ref, g_ref, row_ref = refs[9:]
    for b in range(N_QB):
        d = b % N_Y
        src = own_refs[d] if b < N_Y else other_refs[d]
        for h in range(HEADS):
            cols = slice(h * HD, (h + 1) * HD)
            out = slice((b * HEADS + h) * TOK, (b * HEADS + h + 1) * TOK)
            q_ref[out, :] = src[0:TOK, cols]
            g_ref[out, :] = src[TOK : 2 * TOK, cols]
        aux = src[2 * TOK : ROWS, :].astype(F32)
        cols = slice(b * HEADS * TOK, (b + 1) * HEADS * TOK)
        row_ref[0:1, cols] = (aux[2:3] + aux[1:2]) + aux[0:1]
        row_ref[1:2, cols] = (aux[5:6] + aux[4:5]) + aux[3:4]
        row_ref[2:3, cols] = jnp.concatenate([line_ref[b : b + 1, :]] * HEADS, axis=1)


def slot_of(block):
    d = lax.rem(block - lax.axis_index("z") + N_Z, N_Z)
    low, high = lax.rem(d, 4), d // 4
    flip = jnp.where(low == 3, 1, jnp.where(low == 2, lax.axis_index("core"), 0))
    return low * 2 + lax.rem(high + flip, 2)


def main_kernel(is_last, q_ref, g_ref, row_ref, kv_ref, kpos_ref, *refs):
    if is_last:
        dq_in_ref, dqo_ref, dqs_ref, dkv_ref, kt_ref, dqt_ref = refs
    else:
        dqt_ref, dkv_ref, kt_ref = refs
    for j in range(N_Z):
        rows = slice(j * TOK, (j + 1) * TOK)
        kt_ref[:, rows] = kv_ref[rows, 0:HD].T
    for first in range(0, N_Z * TOK, TILE):
        ks = slice(first, first + TILE)
        k = kv_ref[ks, 0:HD]
        v = kv_ref[ks, HD : 2 * HD]
        kt = kt_ref[:, ks]
        dk = jnp.zeros((TILE, HD), F32)
        dv = jnp.zeros((TILE, HD), F32)
        for b in range(0, N_QB, STEP):
            rs = slice(b * HEADS * TOK, (b + STEP) * HEADS * TOK)
            q = q_ref[rs, :]
            g = g_ref[rs, :]
            s = lax.dot_general(k, q, (((1,), (1,)), ((), ())), preferred_element_type=F32)
            dp = lax.dot_general(v, g, (((1,), (1,)), ((), ())), preferred_element_type=F32)
            keep = []
            for i in range(b, b + STEP):
                at = i * HEADS * TOK
                keep += [row_ref[2:3, at : at + TOK] >= kpos_ref[ks, :]] * HEADS
            p = jnp.where(jnp.concatenate(keep, axis=1), jnp.exp2(s - row_ref[0:1, rs]), 0.0)
            ds = (p * (dp - row_ref[1:2, rs])).astype(BF16)
            dv = dv + jnp.dot(p.astype(BF16), g, preferred_element_type=F32)
            dk = dk + jnp.dot(ds, q, preferred_element_type=F32)
            dq = jnp.dot(kt, ds, preferred_element_type=F32)
            if first > 0:
                dqt_ref[:, rs] += dq
            elif is_last:
                dqt_ref[:, rs] = dq_in_ref[:, rs] + dq
            else:
                dqt_ref[:, rs] = dq
        for i in range(TILE // TOK):
            at = slice(i * TOK, (i + 1) * TOK)
            out = pl.ds(pl.multiple_of(slot_of(first // TOK + i) * TOK, TOK), TOK)
            dkv_ref[out, 0:HD] = (dk[at] * SCALE).astype(BF16)
            dkv_ref[out, HD : 2 * HD] = dv[at].astype(BF16)
    if is_last:
        for b in range(N_QB):
            out = dqo_ref if b < N_Y else dqs_ref
            d = b % N_Y
            for h in range(HEADS):
                at = (b * HEADS + h) * TOK
                blk = dqt_ref[:, at : at + TOK] * LN2
                out[d * TOK : (d + 1) * TOK, h * HD : (h + 1) * HD] = blk.T.astype(BF16)


def whole(*shape):
    return pl.BlockSpec(shape, lambda i: (0,) * len(shape), pipeline_mode=pl.Buffered(1))


def whole_of(x):
    return whole(*x.shape)


PARAMS = pltpu.CompilerParams(vmem_limit_bytes=VMEM_LIMIT)


def plain_call(kernel, out_shape, args):
    return pl.pallas_call(
        kernel,
        in_specs=[VMEM] * len(args),
        out_specs=[VMEM] * len(out_shape),
        out_shape=out_shape,
        compiler_params=pltpu.CompilerParams(vmem_limit_bytes=LOCAL_LIMIT),
        name=kernel.__name__,
    )(*args)


def keep(q_pay, pos):
    keys = N_Z * TOK
    out_shape = [
        jax.ShapeDtypeStruct((ROWS, HEADS * HD), BF16),
        jax.ShapeDtypeStruct((N_QB, TOK), F32),
        jax.ShapeDtypeStruct((keys, TOK), F32),
        jax.ShapeDtypeStruct((keys, TOK), F32),
    ]
    return plain_call(keep_kernel, out_shape, (q_pay, pos))


def stack(own, other, line):
    rows = N_QB * HEADS * TOK
    out_shape = [
        jax.ShapeDtypeStruct((rows, HD), BF16),
        jax.ShapeDtypeStruct((rows, HD), BF16),
        jax.ShapeDtypeStruct((8, rows), F32),
    ]
    return plain_call(stack_kernel, out_shape, (*own, *other, line))


def attend(q, g, row, kv, kpos, dq_in):
    is_last = dq_in is not None
    keys = N_Z * TOK
    rows = N_QB * HEADS * TOK
    dqt = (HD, rows)
    dkv_shape = jax.ShapeDtypeStruct((keys, 2 * HD), BF16)
    scratch = [pltpu.VMEM((HD, keys), BF16)]
    if is_last:
        half = jax.ShapeDtypeStruct((N_Y * TOK, HEADS * HD), BF16)
        out_shape = [half, half, dkv_shape]
        scratch.append(pltpu.VMEM(dqt, F32))
    else:
        out_shape = [jax.ShapeDtypeStruct(dqt, F32), dkv_shape]
    args = [q, g, row, kv, kpos] + ([dq_in] if is_last else [])
    return pl.pallas_call(
        functools.partial(main_kernel, is_last),
        in_specs=[VMEM] * len(args),
        out_specs=[VMEM] * len(out_shape),
        out_shape=out_shape,
        scratch_shapes=scratch,
        compiler_params=pltpu.CompilerParams(vmem_limit_bytes=LOCAL_LIMIT),
        cost_estimate=pl.CostEstimate(
            flops=10 * HD * rows * keys, bytes_accessed=8 * 2**20, transcendentals=rows * keys
        ),
        name="attend",
    )(*args)


def shift_y(x, d):
    return lax.ppermute(x, "y", [(i, (i - d) % N_Y) for i in range(N_Y)])


def swap(x, axis):
    return lax.ppermute(x, axis, [(0, 1), (1, 0)])


def finish_kernel(own_ref, *refs):
    total = own_ref[...]
    for ref in refs[:-1]:
        total = total + ref[...].astype(F32)
    refs[-1][...] = total.astype(BF16)


def finish(own, parts):
    return pl.pallas_call(
        finish_kernel,
        in_specs=[VMEM] * (1 + len(parts)),
        out_specs=VMEM,
        out_shape=jax.ShapeDtypeStruct(own.shape, BF16),
        compiler_params=pltpu.CompilerParams(vmem_limit_bytes=LOCAL_LIMIT),
        cost_estimate=pl.CostEstimate(flops=10**10, bytes_accessed=2**20, transcendentals=0),
        name="finish",
    )(own, *parts)


def move_z(x, by0, by1):
    pairs = [
        (z * N_CORE + c, (z + by) % N_Z * N_CORE + c)
        for z in range(N_Z)
        for c, by in ((0, by0), (1, by1))
    ]
    return lax.ppermute(x, ("z", "core"), pairs)


def cross(x):
    flat = lambda z, core, xl: (z * N_CORE + core) * N_XL + xl
    pairs = [
        (flat(z, c, xl), flat((z + 4) % N_Z, c, 1 - xl))
        for z in range(N_Z)
        for c in range(N_CORE)
        for xl in range(N_XL)
    ]
    return lax.ppermute(x, ("z", "core", "xl"), pairs)


def shards(queries, keys, values, outputs, out_grad, log_norm, positions):
    args = (queries, keys, values, outputs, out_grad, log_norm.T)
    pays = [
        jax.ShapeDtypeStruct((ROWS, HEADS * HD), BF16),
        jax.ShapeDtypeStruct((N_Z * TOK, 2 * HD), BF16),
    ]
    q_pay, kv_send = pl.pallas_call(
        prep_kernel,
        grid=(1,),
        in_specs=[whole_of(x) for x in args],
        out_specs=[whole_of(x) for x in pays],
        out_shape=pays,
        compiler_params=PARAMS,
        name="prep",
    )(*args)
    pos = positions.reshape(-1, TOK)
    own = [q_pay] + [None] * 3
    for d in (1, 3, 2):
        own[d] = shift_y(q_pay, d)
    kv = lax.all_to_all(kv_send, "z", 0, 0, tiled=True)
    mine, line, near, far = keep(q_pay, pos)
    own[3], mine, line, near, far = lax.optimization_barrier((own[3], mine, line, near, far))
    other = [swap(x, "core") for x in own]
    own[0] = mine
    kv_far = swap(kv, "xl")
    q, g, row = stack(own, other, line)
    dqt, dkv = attend(q, g, row, kv, near, None)
    dkv_got = swap(dkv, "xl")
    dq_own, dq_swap, dkv_far = attend(q, g, row, kv_far, far, dqt)
    dq_sum = dq_own.astype(F32) + swap(dq_swap, "core").astype(F32)
    dq_low = dq_sum.astype(BF16).reshape(N_Y, TOK, HEADS * HD)
    dq_got = [shift_y(dq_low[d], N_Y - d) for d in (1, 3, 2)]
    kv_sum = (dkv_far.astype(F32) + dkv_got.astype(F32)).astype(BF16).reshape(4, 2 * TOK, 2 * HD)
    pair = kv_sum[0].astype(F32)
    for part in (move_z(kv_sum[1], 1, 1), move_z(kv_sum[3], -1, -1), move_z(kv_sum[2], 2, -2)):
        pair = pair + part.astype(F32)
    pair = pair.astype(BF16)
    tied = [dq_got[i] for i in (2,)]
    pair, tied = lax.optimization_barrier((pair, tied))
    dq_got = tied + [dq_got[i] for i in (0, 1)]
    dkv = swap(pair[0:TOK], "xl").astype(F32) + cross(pair[TOK : 2 * TOK]).astype(F32)
    dkv = dkv.astype(BF16)
    dq = finish(dq_sum[0:TOK], dq_got)
    return dq, dkv[:, 0:HD], dkv[:, HD : 2 * HD]


def solution(mesh):
    dp = mesh.devices.shape[0]
    grid = Mesh(
        mesh.devices.reshape(dp, N_Z, N_CORE, N_XL, N_Y), ("dp", "z", "core", "xl", "y")
    )
    rows = P(("dp", "z", "core", "xl", "y"), None)
    return jax.shard_map(
        shards,
        mesh=grid,
        in_specs=(rows,) * 6 + (P("dp"),),
        out_specs=(rows,) * 3,
        check_vma=False,
    )
```

```python
import functools
import math

import jax
import jax.numpy as jnp
from jax import lax
from jax.experimental import pallas as pl
from jax.experimental.pallas import tpu as pltpu
from jax.sharding import Mesh, PartitionSpec as P

F32 = jnp.float32
BF16 = jnp.bfloat16

HEADS = 4
HD = 128
TOK = 128
N_Z, N_CORE, N_XL, N_Y = 8, 2, 2, 4
ROWS = 2 * TOK + 16
N_QB = N_CORE * N_Y
TILE = 512
STEP = 4
SCALE = 1.0 / math.sqrt(HD)
LOG2E = math.log2(math.e)
LN2 = math.log(2.0)
VMEM_LIMIT = 60 * 2**20
LOCAL_LIMIT = 24 * 2**20

VMEM = pl.BlockSpec(memory_space=pltpu.VMEM)


def split3(x):
    hi = x.astype(BF16)
    rest = x - hi.astype(F32)
    mid = rest.astype(BF16)
    low = (rest - mid.astype(F32)).astype(BF16)
    return [hi, mid, low]


def prep_kernel(q_ref, k_ref, v_ref, o_ref, g_ref, n_ref, qp_ref, kv_ref):
    qp_ref[0:TOK, :] = q_ref[...]
    qp_ref[TOK : 2 * TOK, :] = g_ref[...]
    key = (k_ref[...].astype(F32) * (SCALE * LOG2E)).astype(BF16)
    for j in range(N_Z):
        kv_ref[j * TOK : (j + 1) * TOK, 0:HD] = key
        kv_ref[j * TOK : (j + 1) * TOK, HD : 2 * HD] = v_ref[...]
    deltas, norms = [], []
    for h in range(HEADS):
        cols = slice(h * HD, (h + 1) * HD)
        prod = g_ref[:, cols].astype(F32) * o_ref[:, cols].astype(F32)
        deltas.append(jnp.sum(prod.T, axis=0, keepdims=True))
        norms.append(n_ref[h : h + 1, :] * LOG2E)
    parts = split3(jnp.concatenate(norms, axis=1)) + split3(jnp.concatenate(deltas, axis=1))
    parts = [p.astype(F32) for p in parts] + [jnp.zeros((10, HEADS * TOK), F32)]
    qp_ref[2 * TOK : ROWS, :] = jnp.concatenate(parts, axis=0).astype(BF16)


def keep_kernel(pay_ref, pos_ref, keep_ref, line_ref, near_ref, far_ref):
    keep_ref[...] = pay_ref[...]
    z, core, xl, y = (lax.axis_index(a) for a in ("z", "core", "xl", "y"))
    for b in range(N_QB):
        owner = core if b < N_Y else 1 - core
        block = z * 16 + owner * 8 + xl * 4 + lax.rem(y + b % N_Y, N_Y)
        line_ref[b : b + 1, :] = pos_ref[pl.ds(block, 1), :].astype(F32)
    for j in range(N_Z):
        for column, out in ((xl, near_ref), (1 - xl, far_ref)):
            block = j * 16 + core * 8 + column * 4 + y
            line = pos_ref[pl.ds(block, 1), :].astype(F32)
            out[j * TOK : (j + 1) * TOK, :] = jnp.broadcast_to(line, (TOK, TOK)).T


def stack_kernel(*refs):
    own_refs, other_refs, line_ref = refs[0:4], refs[4:8], refs[8]
    q_ref, g_ref, row_ref = refs[9:]
    for b in range(N_QB):
        d = b % N_Y
        src = own_refs[d] if b < N_Y else other_refs[d]
        for h in range(HEADS):
            cols = slice(h * HD, (h + 1) * HD)
            out = slice((b * HEADS + h) * TOK, (b * HEADS + h + 1) * TOK)
            q_ref[out, :] = src[0:TOK, cols]
            g_ref[out, :] = src[TOK : 2 * TOK, cols]
        aux = src[2 * TOK : ROWS, :].astype(F32)
        cols = slice(b * HEADS * TOK, (b + 1) * HEADS * TOK)
        row_ref[0:1, cols] = (aux[2:3] + aux[1:2]) + aux[0:1]
        row_ref[1:2, cols] = (aux[5:6] + aux[4:5]) + aux[3:4]
        row_ref[2:3, cols] = jnp.concatenate([line_ref[b : b + 1, :]] * HEADS, axis=1)


def slot_of(block):
    d = lax.rem(block - lax.axis_index("z") + N_Z, N_Z)
    low, high = lax.rem(d, 4), d // 4
    flip = jnp.where(low == 3, 1, jnp.where(low == 2, lax.axis_index("core"), 0))
    return low * 2 + lax.rem(high + flip, 2)


def main_kernel(is_last, q_ref, g_ref, row_ref, kv_ref, kpos_ref, *refs):
    if is_last:
        dq_in_ref, dqo_ref, dqs_ref, dkv_ref, kt_ref, dqt_ref = refs
    else:
        dqt_ref, dkv_ref, kt_ref = refs
    for j in range(N_Z):
        rows = slice(j * TOK, (j + 1) * TOK)
        kt_ref[:, rows] = kv_ref[rows, 0:HD].T
    for first in range(0, N_Z * TOK, TILE):
        ks = slice(first, first + TILE)
        k = kv_ref[ks, 0:HD]
        v = kv_ref[ks, HD : 2 * HD]
        kt = kt_ref[:, ks]
        dk = jnp.zeros((TILE, HD), F32)
        dv = jnp.zeros((TILE, HD), F32)
        for b in range(0, N_QB, STEP):
            rs = slice(b * HEADS * TOK, (b + STEP) * HEADS * TOK)
            q = q_ref[rs, :]
            g = g_ref[rs, :]
            s = lax.dot_general(k, q, (((1,), (1,)), ((), ())), preferred_element_type=F32)
            dp = lax.dot_general(v, g, (((1,), (1,)), ((), ())), preferred_element_type=F32)
            keep = []
            for i in range(b, b + STEP):
                at = i * HEADS * TOK
                keep += [row_ref[2:3, at : at + TOK] >= kpos_ref[ks, :]] * HEADS
            p = jnp.where(jnp.concatenate(keep, axis=1), jnp.exp2(s - row_ref[0:1, rs]), 0.0)
            ds = (p * (dp - row_ref[1:2, rs])).astype(BF16)
            dv = dv + jnp.dot(p.astype(BF16), g, preferred_element_type=F32)
            dk = dk + jnp.dot(ds, q, preferred_element_type=F32)
            dq = jnp.dot(kt, ds, preferred_element_type=F32)
            if first > 0:
                dqt_ref[:, rs] += dq
            elif is_last:
                dqt_ref[:, rs] = dq_in_ref[:, rs] + dq
            else:
                dqt_ref[:, rs] = dq
        for i in range(TILE // TOK):
            at = slice(i * TOK, (i + 1) * TOK)
            out = pl.ds(pl.multiple_of(slot_of(first // TOK + i) * TOK, TOK), TOK)
            dkv_ref[out, 0:HD] = (dk[at] * SCALE).astype(BF16)
            dkv_ref[out, HD : 2 * HD] = dv[at].astype(BF16)
    if is_last:
        for b in range(N_QB):
            out = dqo_ref if b < N_Y else dqs_ref
            d = b % N_Y
            for h in range(HEADS):
                at = (b * HEADS + h) * TOK
                blk = dqt_ref[:, at : at + TOK] * LN2
                out[d * TOK : (d + 1) * TOK, h * HD : (h + 1) * HD] = blk.T.astype(BF16)


def whole(*shape):
    return pl.BlockSpec(shape, lambda i: (0,) * len(shape), pipeline_mode=pl.Buffered(1))


def whole_of(x):
    return whole(*x.shape)


PARAMS = pltpu.CompilerParams(vmem_limit_bytes=VMEM_LIMIT)


def plain_call(kernel, out_shape, args):
    return pl.pallas_call(
        kernel,
        in_specs=[VMEM] * len(args),
        out_specs=[VMEM] * len(out_shape),
        out_shape=out_shape,
        compiler_params=pltpu.CompilerParams(vmem_limit_bytes=LOCAL_LIMIT),
        name=kernel.__name__,
    )(*args)


def keep(q_pay, pos):
    keys = N_Z * TOK
    out_shape = [
        jax.ShapeDtypeStruct((ROWS, HEADS * HD), BF16),
        jax.ShapeDtypeStruct((N_QB, TOK), F32),
        jax.ShapeDtypeStruct((keys, TOK), F32),
        jax.ShapeDtypeStruct((keys, TOK), F32),
    ]
    return plain_call(keep_kernel, out_shape, (q_pay, pos))


def stack(own, other, line):
    rows = N_QB * HEADS * TOK
    out_shape = [
        jax.ShapeDtypeStruct((rows, HD), BF16),
        jax.ShapeDtypeStruct((rows, HD), BF16),
        jax.ShapeDtypeStruct((8, rows), F32),
    ]
    return plain_call(stack_kernel, out_shape, (*own, *other, line))


def attend(q, g, row, kv, kpos, dq_in):
    is_last = dq_in is not None
    keys = N_Z * TOK
    rows = N_QB * HEADS * TOK
    dqt = (HD, rows)
    dkv_shape = jax.ShapeDtypeStruct((keys, 2 * HD), BF16)
    scratch = [pltpu.VMEM((HD, keys), BF16)]
    if is_last:
        half = jax.ShapeDtypeStruct((N_Y * TOK, HEADS * HD), BF16)
        out_shape = [half, half, dkv_shape]
        scratch.append(pltpu.VMEM(dqt, F32))
    else:
        out_shape = [jax.ShapeDtypeStruct(dqt, F32), dkv_shape]
    args = [q, g, row, kv, kpos] + ([dq_in] if is_last else [])
    return pl.pallas_call(
        functools.partial(main_kernel, is_last),
        in_specs=[VMEM] * len(args),
        out_specs=[VMEM] * len(out_shape),
        out_shape=out_shape,
        scratch_shapes=scratch,
        compiler_params=pltpu.CompilerParams(vmem_limit_bytes=LOCAL_LIMIT),
        cost_estimate=pl.CostEstimate(
            flops=10 * HD * rows * keys, bytes_accessed=8 * 2**20, transcendentals=rows * keys
        ),
        name="attend",
    )(*args)


def shift_y(x, d):
    return lax.ppermute(x, "y", [(i, (i - d) % N_Y) for i in range(N_Y)])


def swap(x, axis):
    return lax.ppermute(x, axis, [(0, 1), (1, 0)])


def finish_kernel(own_ref, *refs):
    total = own_ref[...]
    for ref in refs[:-1]:
        total = total + ref[...].astype(F32)
    refs[-1][...] = total.astype(BF16)


def finish(own, parts):
    return pl.pallas_call(
        finish_kernel,
        in_specs=[VMEM] * (1 + len(parts)),
        out_specs=VMEM,
        out_shape=jax.ShapeDtypeStruct(own.shape, BF16),
        compiler_params=pltpu.CompilerParams(vmem_limit_bytes=LOCAL_LIMIT),
        cost_estimate=pl.CostEstimate(flops=10**10, bytes_accessed=2**20, transcendentals=0),
        name="finish",
    )(own, *parts)


def move_z(x, by0, by1):
    pairs = [
        (z * N_CORE + c, (z + by) % N_Z * N_CORE + c)
        for z in range(N_Z)
        for c, by in ((0, by0), (1, by1))
    ]
    return lax.ppermute(x, ("z", "core"), pairs)


def cross(x):
    flat = lambda z, core, xl: (z * N_CORE + core) * N_XL + xl
    pairs = [
        (flat(z, c, xl), flat((z + 4) % N_Z, c, 1 - xl))
        for z in range(N_Z)
        for c in range(N_CORE)
        for xl in range(N_XL)
    ]
    return lax.ppermute(x, ("z", "core", "xl"), pairs)


def shards(queries, keys, values, outputs, out_grad, log_norm, positions):
    args = (queries, keys, values, outputs, out_grad, log_norm.T)
    pays = [
        jax.ShapeDtypeStruct((ROWS, HEADS * HD), BF16),
        jax.ShapeDtypeStruct((N_Z * TOK, 2 * HD), BF16),
    ]
    q_pay, kv_send = pl.pallas_call(
        prep_kernel,
        grid=(1,),
        in_specs=[whole_of(x) for x in args],
        out_specs=[whole_of(x) for x in pays],
        out_shape=pays,
        compiler_params=PARAMS,
        name="prep",
    )(*args)
    pos = positions.reshape(-1, TOK)
    own = [q_pay] + [None] * 3
    for d in (1, 3, 2):
        own[d] = shift_y(q_pay, d)
    kv = lax.all_to_all(kv_send, "z", 0, 0, tiled=True)
    mine, line, near, far = keep(q_pay, pos)
    own[3], mine, line, near, far = lax.optimization_barrier((own[3], mine, line, near, far))
    other = [swap(x, "core") for x in own]
    own[0] = mine
    kv_far = swap(kv, "xl")
    q, g, row = stack(own, other, line)
    dqt, dkv = attend(q, g, row, kv, near, None)
    dkv_got = swap(dkv, "xl")
    dq_own, dq_swap, dkv_far = attend(q, g, row, kv_far, far, dqt)
    dq_sum = dq_own.astype(F32) + swap(dq_swap, "core").astype(F32)
    dq_low = dq_sum.astype(BF16).reshape(N_Y, TOK, HEADS * HD)
    dq_got = [shift_y(dq_low[d], N_Y - d) for d in (1, 3, 2)]
    kv_sum = (dkv_far.astype(F32) + dkv_got.astype(F32)).astype(BF16).reshape(4, 2 * TOK, 2 * HD)
    pair = kv_sum[0].astype(F32)
    for part in (move_z(kv_sum[1], 1, 1), move_z(kv_sum[3], -1, -1), move_z(kv_sum[2], 2, -2)):
        pair = pair + part.astype(F32)
    pair = pair.astype(BF16)
    tied = [dq_got[i] for i in (2,)]
    pair, tied = lax.optimization_barrier((pair, tied))
    dq_got = tied + [dq_got[i] for i in (0, 1)]
    far = cross(pair[TOK : 2 * TOK])
    dkv = far.astype(F32) + swap(pair[0:TOK], "xl").astype(F32)
    dkv = dkv.astype(BF16)
    dq = finish(dq_sum[0:TOK], dq_got)
    return dq, dkv[:, 0:HD], dkv[:, HD : 2 * HD]


def solution(mesh):
    dp = mesh.devices.shape[0]
    grid = Mesh(
        mesh.devices.reshape(dp, N_Z, N_CORE, N_XL, N_Y), ("dp", "z", "core", "xl", "y")
    )
    rows = P(("dp", "z", "core", "xl", "y"), None)
    return jax.shard_map(
        shards,
        mesh=grid,
        in_specs=(rows,) * 6 + (P("dp"),),
        out_specs=(rows,) * 3,
        check_vma=False,
    )
```

```python
import functools
import math

import jax
import jax.numpy as jnp
from jax import lax
from jax.experimental import pallas as pl
from jax.experimental.pallas import tpu as pltpu
from jax.sharding import Mesh, PartitionSpec as P

F32 = jnp.float32
BF16 = jnp.bfloat16

HEADS = 4
HD = 128
TOK = 128
N_Z, N_CORE, N_XL, N_Y = 8, 2, 2, 4
ROWS = 2 * TOK + 16
N_QB = N_CORE * N_Y
TILE = 512
STEP = 4
SCALE = 1.0 / math.sqrt(HD)
LOG2E = math.log2(math.e)
LN2 = math.log(2.0)
VMEM_LIMIT = 60 * 2**20
LOCAL_LIMIT = 24 * 2**20

VMEM = pl.BlockSpec(memory_space=pltpu.VMEM)


def split3(x):
    hi = x.astype(BF16)
    rest = x - hi.astype(F32)
    mid = rest.astype(BF16)
    low = (rest - mid.astype(F32)).astype(BF16)
    return [hi, mid, low]


def prep_kernel(q_ref, k_ref, v_ref, o_ref, g_ref, n_ref, qp_ref, kv_ref):
    qp_ref[0:TOK, :] = q_ref[...]
    qp_ref[TOK : 2 * TOK, :] = g_ref[...]
    key = (k_ref[...].astype(F32) * (SCALE * LOG2E)).astype(BF16)
    for j in range(N_Z):
        kv_ref[j * TOK : (j + 1) * TOK, 0:HD] = key
        kv_ref[j * TOK : (j + 1) * TOK, HD : 2 * HD] = v_ref[...]
    deltas, norms = [], []
    for h in range(HEADS):
        cols = slice(h * HD, (h + 1) * HD)
        prod = g_ref[:, cols].astype(F32) * o_ref[:, cols].astype(F32)
        deltas.append(jnp.sum(prod.T, axis=0, keepdims=True))
        norms.append(jnp.clip(n_ref[h : h + 1, :] * LOG2E, -1e38, 1e38))
    parts = split3(jnp.concatenate(norms, axis=1)) + split3(jnp.concatenate(deltas, axis=1))
    parts = [p.astype(F32) for p in parts] + [jnp.zeros((10, HEADS * TOK), F32)]
    qp_ref[2 * TOK : ROWS, :] = jnp.concatenate(parts, axis=0).astype(BF16)


def keep_kernel(pay_ref, pos_ref, keep_ref, line_ref, near_ref, far_ref):
    keep_ref[...] = pay_ref[...]
    z, core, xl, y = (lax.axis_index(a) for a in ("z", "core", "xl", "y"))
    for b in range(N_QB):
        owner = core if b < N_Y else 1 - core
        block = z * 16 + owner * 8 + xl * 4 + lax.rem(y + b % N_Y, N_Y)
        line_ref[b : b + 1, :] = pos_ref[pl.ds(block, 1), :].astype(F32)
    for j in range(N_Z):
        for column, out in ((xl, near_ref), (1 - xl, far_ref)):
            block = j * 16 + core * 8 + column * 4 + y
            line = pos_ref[pl.ds(block, 1), :].astype(F32)
            out[j * TOK : (j + 1) * TOK, :] = jnp.broadcast_to(line, (TOK, TOK)).T


def stack_kernel(*refs):
    own_refs, other_refs, line_ref = refs[0:4], refs[4:8], refs[8]
    q_ref, g_ref, row_ref = refs[9:]
    for b in range(N_QB):
        d = b % N_Y
        src = own_refs[d] if b < N_Y else other_refs[d]
        for h in range(HEADS):
            cols = slice(h * HD, (h + 1) * HD)
            out = slice((b * HEADS + h) * TOK, (b * HEADS + h + 1) * TOK)
            q_ref[out, :] = src[0:TOK, cols]
            g_ref[out, :] = src[TOK : 2 * TOK, cols]
        aux = src[2 * TOK : ROWS, :].astype(F32)
        cols = slice(b * HEADS * TOK, (b + 1) * HEADS * TOK)
        row_ref[0:1, cols] = (aux[2:3] + aux[1:2]) + aux[0:1]
        row_ref[1:2, cols] = (aux[5:6] + aux[4:5]) + aux[3:4]
        row_ref[2:3, cols] = jnp.concatenate([line_ref[b : b + 1, :]] * HEADS, axis=1)


def slot_of(block):
    d = lax.rem(block - lax.axis_index("z") + N_Z, N_Z)
    low, high = lax.rem(d, 4), d // 4
    flip = jnp.where(low == 3, 1, jnp.where(low == 2, lax.axis_index("core"), 0))
    return low * 2 + lax.rem(high + flip, 2)


def main_kernel(is_last, q_ref, g_ref, row_ref, kv_ref, kpos_ref, *refs):
    if is_last:
        dq_in_ref, dqo_ref, dqs_ref, dkv_ref, kt_ref, dqt_ref = refs
    else:
        dqt_ref, dkv_ref, kt_ref = refs
    for j in range(N_Z):
        rows = slice(j * TOK, (j + 1) * TOK)
        kt_ref[:, rows] = kv_ref[rows, 0:HD].T
    for first in range(0, N_Z * TOK, TILE):
        ks = slice(first, first + TILE)
        k = kv_ref[ks, 0:HD]
        v = kv_ref[ks, HD : 2 * HD]
        kt = kt_ref[:, ks]
        dk = jnp.zeros((TILE, HD), F32)
        dv = jnp.zeros((TILE, HD), F32)
        for b in range(0, N_QB, STEP):
            rs = slice(b * HEADS * TOK, (b + STEP) * HEADS * TOK)
            q = q_ref[rs, :]
            g = g_ref[rs, :]
            s = lax.dot_general(k, q, (((1,), (1,)), ((), ())), preferred_element_type=F32)
            dp = lax.dot_general(v, g, (((1,), (1,)), ((), ())), preferred_element_type=F32)
            keep = []
            for i in range(b, b + STEP):
                at = i * HEADS * TOK
                keep += [row_ref[2:3, at : at + TOK] >= kpos_ref[ks, :]] * HEADS
            p = jnp.where(jnp.concatenate(keep, axis=1), jnp.exp2(s - row_ref[0:1, rs]), 0.0)
            ds = (p * (dp - row_ref[1:2, rs])).astype(BF16)
            dv = dv + jnp.dot(p.astype(BF16), g, preferred_element_type=F32)
            dk = dk + jnp.dot(ds, q, preferred_element_type=F32)
            dq = jnp.dot(kt, ds, preferred_element_type=F32)
            if first > 0:
                dqt_ref[:, rs] += dq
            elif is_last:
                dqt_ref[:, rs] = dq_in_ref[:, rs] + dq
            else:
                dqt_ref[:, rs] = dq
        for i in range(TILE // TOK):
            at = slice(i * TOK, (i + 1) * TOK)
            out = pl.ds(pl.multiple_of(slot_of(first // TOK + i) * TOK, TOK), TOK)
            dkv_ref[out, 0:HD] = (dk[at] * SCALE).astype(BF16)
            dkv_ref[out, HD : 2 * HD] = dv[at].astype(BF16)
    if is_last:
        for b in range(N_QB):
            out = dqo_ref if b < N_Y else dqs_ref
            d = b % N_Y
            for h in range(HEADS):
                at = (b * HEADS + h) * TOK
                blk = dqt_ref[:, at : at + TOK] * LN2
                out[d * TOK : (d + 1) * TOK, h * HD : (h + 1) * HD] = blk.T.astype(BF16)


def whole(*shape):
    return pl.BlockSpec(shape, lambda i: (0,) * len(shape), pipeline_mode=pl.Buffered(1))


def whole_of(x):
    return whole(*x.shape)


PARAMS = pltpu.CompilerParams(vmem_limit_bytes=VMEM_LIMIT)


def plain_call(kernel, out_shape, args):
    return pl.pallas_call(
        kernel,
        in_specs=[VMEM] * len(args),
        out_specs=[VMEM] * len(out_shape),
        out_shape=out_shape,
        compiler_params=pltpu.CompilerParams(vmem_limit_bytes=LOCAL_LIMIT),
        name=kernel.__name__,
    )(*args)


def keep(q_pay, pos):
    keys = N_Z * TOK
    out_shape = [
        jax.ShapeDtypeStruct((ROWS, HEADS * HD), BF16),
        jax.ShapeDtypeStruct((N_QB, TOK), F32),
        jax.ShapeDtypeStruct((keys, TOK), F32),
        jax.ShapeDtypeStruct((keys, TOK), F32),
    ]
    return plain_call(keep_kernel, out_shape, (q_pay, pos))


def stack(own, other, line):
    rows = N_QB * HEADS * TOK
    out_shape = [
        jax.ShapeDtypeStruct((rows, HD), BF16),
        jax.ShapeDtypeStruct((rows, HD), BF16),
        jax.ShapeDtypeStruct((8, rows), F32),
    ]
    return plain_call(stack_kernel, out_shape, (*own, *other, line))


def attend(q, g, row, kv, kpos, dq_in):
    is_last = dq_in is not None
    keys = N_Z * TOK
    rows = N_QB * HEADS * TOK
    dqt = (HD, rows)
    dkv_shape = jax.ShapeDtypeStruct((keys, 2 * HD), BF16)
    scratch = [pltpu.VMEM((HD, keys), BF16)]
    if is_last:
        half = jax.ShapeDtypeStruct((N_Y * TOK, HEADS * HD), BF16)
        out_shape = [half, half, dkv_shape]
        scratch.append(pltpu.VMEM(dqt, F32))
    else:
        out_shape = [jax.ShapeDtypeStruct(dqt, F32), dkv_shape]
    args = [q, g, row, kv, kpos] + ([dq_in] if is_last else [])
    return pl.pallas_call(
        functools.partial(main_kernel, is_last),
        in_specs=[VMEM] * len(args),
        out_specs=[VMEM] * len(out_shape),
        out_shape=out_shape,
        scratch_shapes=scratch,
        compiler_params=pltpu.CompilerParams(vmem_limit_bytes=LOCAL_LIMIT),
        cost_estimate=pl.CostEstimate(
            flops=10 * HD * rows * keys, bytes_accessed=8 * 2**20, transcendentals=rows * keys
        ),
        name="attend",
    )(*args)


def shift_y(x, d):
    return lax.ppermute(x, "y", [(i, (i - d) % N_Y) for i in range(N_Y)])


def swap(x, axis):
    return lax.ppermute(x, axis, [(0, 1), (1, 0)])


def finish_kernel(own_ref, *refs):
    total = own_ref[...]
    for ref in refs[:-1]:
        total = total + ref[...].astype(F32)
    refs[-1][...] = total.astype(BF16)


def finish(own, parts):
    return pl.pallas_call(
        finish_kernel,
        in_specs=[VMEM] * (1 + len(parts)),
        out_specs=VMEM,
        out_shape=jax.ShapeDtypeStruct(own.shape, BF16),
        compiler_params=pltpu.CompilerParams(vmem_limit_bytes=LOCAL_LIMIT),
        cost_estimate=pl.CostEstimate(flops=10**10, bytes_accessed=2**20, transcendentals=0),
        name="finish",
    )(own, *parts)


def move_z(x, by0, by1):
    pairs = [
        (z * N_CORE + c, (z + by) % N_Z * N_CORE + c)
        for z in range(N_Z)
        for c, by in ((0, by0), (1, by1))
    ]
    return lax.ppermute(x, ("z", "core"), pairs)


def cross(x):
    flat = lambda z, core, xl: (z * N_CORE + core) * N_XL + xl
    pairs = [
        (flat(z, c, xl), flat((z + 4) % N_Z, c, 1 - xl))
        for z in range(N_Z)
        for c in range(N_CORE)
        for xl in range(N_XL)
    ]
    return lax.ppermute(x, ("z", "core", "xl"), pairs)


def shards(queries, keys, values, outputs, out_grad, log_norm, positions):
    args = (queries, keys, values, outputs, out_grad, log_norm.T)
    pays = [
        jax.ShapeDtypeStruct((ROWS, HEADS * HD), BF16),
        jax.ShapeDtypeStruct((N_Z * TOK, 2 * HD), BF16),
    ]
    q_pay, kv_send = pl.pallas_call(
        prep_kernel,
        grid=(1,),
        in_specs=[whole_of(x) for x in args],
        out_specs=[whole_of(x) for x in pays],
        out_shape=pays,
        compiler_params=PARAMS,
        name="prep",
    )(*args)
    pos = positions.reshape(-1, TOK)
    own = [q_pay] + [None] * 3
    for d in (1, 3, 2):
        own[d] = shift_y(q_pay, d)
    kv = lax.all_to_all(kv_send, "z", 0, 0, tiled=True)
    mine, line, near, far = keep(q_pay, pos)
    own[3], mine, line, near, far = lax.optimization_barrier((own[3], mine, line, near, far))
    other = [swap(x, "core") for x in own]
    own[0] = mine
    kv_far = swap(kv, "xl")
    q, g, row = stack(own, other, line)
    dqt, dkv = attend(q, g, row, kv, near, None)
    dkv_got = swap(dkv, "xl")
    dq_own, dq_swap, dkv_far = attend(q, g, row, kv_far, far, dqt)
    dq_sum = dq_own.astype(F32) + swap(dq_swap, "core").astype(F32)
    dq_low = dq_sum.astype(BF16).reshape(N_Y, TOK, HEADS * HD)
    dq_got = [shift_y(dq_low[d], N_Y - d) for d in (1, 3, 2)]
    kv_sum = (dkv_far.astype(F32) + dkv_got.astype(F32)).astype(BF16).reshape(4, 2 * TOK, 2 * HD)
    pair = kv_sum[0].astype(F32)
    for part in (move_z(kv_sum[1], 1, 1), move_z(kv_sum[3], -1, -1), move_z(kv_sum[2], 2, -2)):
        pair = pair + part.astype(F32)
    pair = pair.astype(BF16)
    tied = [dq_got[i] for i in (2,)]
    pair, tied = lax.optimization_barrier((pair, tied))
    dq_got = tied + [dq_got[i] for i in (0, 1)]
    far = cross(pair[TOK : 2 * TOK])
    dkv = far.astype(F32) + swap(pair[0:TOK], "xl").astype(F32)
    dkv = dkv.astype(BF16)
    dq = finish(dq_sum[0:TOK], dq_got)
    return dq, dkv[:, 0:HD], dkv[:, HD : 2 * HD]


def solution(mesh):
    dp = mesh.devices.shape[0]
    grid = Mesh(
        mesh.devices.reshape(dp, N_Z, N_CORE, N_XL, N_Y), ("dp", "z", "core", "xl", "y")
    )
    rows = P(("dp", "z", "core", "xl", "y"), None)
    return jax.shard_map(
        shards,
        mesh=grid,
        in_specs=(rows,) * 6 + (P("dp"),),
        out_specs=(rows,) * 3,
        check_vma=False,
    )
```
